256 devices in a mesh: img: 64 (over z, x, core), hid: 4 (over y).
Axes of the slice: x: 4, y: 4, z: 8, core: 2. Of those that a mesh axis runs over, the one named last changes fastest.
Arguments:
- patches: bfloat16 [32768, 6144], P('img'), may hold values from -6 to 6
- hidden_grads: bfloat16 [32768, 24576], P('img', 'hid'), may hold values from -0.5 to 0.5
- proj_in: bfloat16 [6144, 128], replicated, may hold values from -0.078125 to 0.078125
- proj_out: bfloat16 [24576, 128], P('hid'), may hold values from -0.0390625 to 0.0390625
- slot_image: int32 [128], P('img'), may hold values from 0 to 127, each once
- patch_counts: int32 [128], P('img'), may hold values from 128 to 256, as said below
Outputs:
- sketches: float32 [16384, 128], P(('img', 'hid'))
The draws below stay inside these ranges and needn't reach their ends.
Inputs may be any that keep to these rules, and one draw needn't show every extreme that they name: `slot_image`: each value names one image's slot; every image has exactly one slot. `patch_counts`: the counts of one packing block sum to at most 512; some block is full.
All inputs are finite; a program needn't handle non-finite values.
Results may differ from the reference program's by a relative error of at most 0.0003.
Values sent between devices are 32-bit elements; how exact they have to be, the bound alone decides.
A program may use at most 128 MiB of HBM per device.

```python
import jax
import jax.numpy as jnp
from jax import lax

D = 6144
MLP = 24576
K = 128
MOST = 256
IMG_DEV = 2
ROW_DEV = 512
IMAGES = 128
ROWS = 32768
N_IMG = 64


def draw_patch_counts(key, part):
    key = jax.random.fold_in(key, 7)
    first, second = jax.random.split(key)
    counts = jax.random.randint(first, (IMAGES,), MOST // 2, MOST + 1, dtype=jnp.int32)
    block = jax.random.randint(second, (), 0, N_IMG, dtype=jnp.int32)
    slot_ids = jnp.arange(IMAGES, dtype=jnp.int32)
    full = slot_ids // IMG_DEV == block
    return jnp.where(full, MOST, counts).astype(jnp.int32)


def shard_levels(stream_key, extent, cuts, least, high):
    factor_of, own = 1.0, jax.random.fold_in(stream_key, 6)
    for dim, shards_of in cuts:
        heights = jnp.exp(jax.random.uniform(jax.random.fold_in(own, dim), (shards_of,), jnp.float32, least / len(cuts), high / len(cuts)))
        factor_of = factor_of * jnp.repeat(heights, extent[dim] // shards_of).reshape([-1 if axis == dim else 1 for axis in range(len(extent))])
    return factor_of


def centred(rng, extent, spread, most, pieces=(), held_as=jnp.bfloat16):
    array = jax.random.normal(rng, extent, jnp.float32) * spread
    if len(pieces) > 0:
        array = shard_levels(rng, extent, pieces, -0.22, 0.18) * array
    return jnp.clip(array, min=-most, max=most).astype(held_as)


def setup_inputs(seed: int = 0) -> dict:
    seeds = jax.random.split(jax.random.key(seed), 7)
    patches = centred(seeds[0], (ROWS, D), 1.0, 6.0, ((0, 64),))
    hidden_grads = centred(seeds[1], (ROWS, MLP), 0.07, 0.5, ((0, 64), (1, 4)))
    proj_in = centred(seeds[2], (D, K), D ** -0.5, 0.078125)
    proj_out = centred(seeds[3], (MLP, K), MLP ** -0.5, 0.0390625, ((0, 4),))
    slot_image = jax.random.permutation(seeds[4], IMAGES).astype(jnp.int32)
    patch_counts = draw_patch_counts(jax.random.fold_in(seeds[6], 71), 0)
    return {"patches": patches, "hidden_grads": hidden_grads, "proj_in": proj_in, "proj_out": proj_out, "slot_image": slot_image, "patch_counts": patch_counts}


def block_sketch(args, proj_in, proj_out):
    rows_x, rows_g, counts = args
    reduced = jnp.dot(rows_x, proj_in, preferred_element_type=jnp.float32)
    projected = jnp.dot(rows_g, proj_out, preferred_element_type=jnp.float32)
    starts = jnp.cumsum(counts) - counts
    position = jnp.arange(ROW_DEV, dtype=jnp.int32)
    member = ((position[None, :] >= starts[:, None]) & (position[None, :] < (starts + counts)[:, None])).astype(jnp.float32)
    masked = member[:, :, None] * reduced[None, :, :]
    return jnp.einsum("srk,rl->skl", masked, projected, precision=lax.Precision.HIGHEST)


def reference(patches, hidden_grads, proj_in, proj_out, slot_image, patch_counts):
    xs = patches.reshape(N_IMG, ROW_DEV, D)
    gs = hidden_grads.reshape(N_IMG, ROW_DEV, MLP)
    cs = patch_counts.reshape(N_IMG, IMG_DEV)
    slot_sketch = lax.map(lambda item: block_sketch(item, proj_in, proj_out), (xs, gs, cs))
    slot_sketch = slot_sketch.reshape(IMAGES, K, K)
    placed = jnp.zeros((IMAGES, K, K), jnp.float32).at[slot_image].set(slot_sketch)
    return placed.reshape(IMAGES * K, K)
```

```python
import functools

import jax
import jax.numpy as jnp
from jax import lax
from jax.experimental import pallas as pl
from jax.experimental.pallas import tpu as pltpu
from jax.sharding import PartitionSpec as P

MESH = pl.DeviceIdType.MESH
XC = 8
CHUNK = 128


def far_first(n):
    return sorted(range(1, n), key=lambda o: -min(o, n - o))


def split(v):
    hi = v.astype(jnp.bfloat16)
    lo = (v - hi.astype(jnp.float32)).astype(jnp.bfloat16)
    return hi, lo


def kernel(nz, ny, image_ref, count_ref, x_hbm, g_hbm, wi_hbm, wo_hbm, out_ref,
           xv, gv, wi, wo, red, prj, part, gath, ring, pick, idrow, idxc, idz, where_smem,
           x_sem, g_sem, w_sem, id_send, id_recv, idz_send, idz_recv,
           p1_send, p1_recv, ag_send, ag_recv, p3_send, p3_recv):
    b, y = lax.axis_index("img"), lax.axis_index("hid")
    z, xc = b // XC, b % XC
    rows, depth = xv.shape
    kw, lw = wi.shape[1], wo.shape[1]
    half_rows = rows // 2
    npiece = ny * XC
    t = kw // npiece
    chunks = rows // CHUNK
    f32 = jnp.float32

    def dev(zz, cc, yy):
        return (zz * XC + cc, yy)

    loads = []
    w_in = pltpu.make_async_copy(wi_hbm, wi, w_sem.at[0])
    w_out = pltpu.make_async_copy(wo_hbm, wo, w_sem.at[1])

    def x_copy(i):
        return pltpu.make_async_copy(x_hbm.at[pl.ds(i * CHUNK, CHUNK)], xv.at[pl.ds(i * CHUNK, CHUNK)], x_sem.at[i])

    def g_copy(i):
        return pltpu.make_async_copy(g_hbm.at[pl.ds(i * CHUNK, CHUNK)], gv.at[pl.ds(i * CHUNK, CHUNK)], g_sem.at[i])

    w_in.start()
    x_copy(0).start()
    w_out.start()
    g_copy(0).start()
    for i in range(1, chunks):
        x_copy(i).start()
        g_copy(i).start()

    group = [(oc, oy) for oy in [0] + far_first(ny) for oc in [0] + far_first(XC) if (oc, oy) != (0, 0)]
    group.sort(key=lambda o: -(min(o[0] // 2, XC // 2 - o[0] // 2) + min(o[1], ny - o[1])))
    barrier = pltpu.get_barrier_semaphore()
    for oc, oy in group:
        pl.semaphore_signal(barrier, inc=1, device_id=dev(z, (xc + oc) % XC, (y + oy) % ny), device_id_type=MESH)
    for oz in far_first(nz):
        pl.semaphore_signal(barrier, inc=1, device_id=dev((z + oz) % nz, xc, y), device_id_type=MESH)

    slots = 2 * nz * XC
    lane = lax.broadcasted_iota(jnp.int32, (8, 128), 1)
    first, second = image_ref[0], image_ref[1]
    idrow[...] = jnp.where(lane == b, first, jnp.where(lane == slots // 2 + b, second, 0))

    c0, c1 = count_ref[0], count_ref[1]

    def project(i):
        r = pl.ds(pl.multiple_of(i * CHUNK, CHUNK), CHUNK)
        x_copy(i).wait()
        red[r, :] = jnp.dot(xv[r, :], wi[...], preferred_element_type=f32)
        g_copy(i).wait()
        prj[r, :] = jnp.dot(gv[r, :], wo[...], preferred_element_type=f32)

    def members(h):
        pos = lax.broadcasted_iota(jnp.int32, (half_rows, lw), 0) + h * half_rows
        return pos < c0, (pos >= c0) & (pos < c0 + c1)

    def sketch(h, masks):
        r = pl.ds(h * half_rows, half_rows)
        a = jnp.concatenate(split(red[r, :].T), axis=0)
        hi, lo = split(prj[r, :])
        zero = jnp.zeros_like(hi)
        rhs = jnp.concatenate([jnp.where(m, v, zero) for m in masks for v in (hi, lo)], axis=1)
        full = jnp.dot(a, rhs, preferred_element_type=f32)
        return [
            full[:kw, 2 * lw * j : 2 * lw * j + lw]
            + (full[:kw, 2 * lw * j + lw : 2 * lw * (j + 1)] + full[kw:, 2 * lw * j : 2 * lw * j + lw])
            for j in range(len(masks))
        ]

    def put(s, value):
        for i in range(npiece):
            part[s, i] = value[i * t : (i + 1) * t]

    def scatter(s):
        pltpu.make_async_copy(part.at[s, y * XC + xc], gath.at[s, y, xc], p1_recv.at[s]).start()
        for oc, oy in group:
            cc, yy = (xc + oc) % XC, (y + oy) % ny
            pltpu.make_async_remote_copy(
                src_ref=part.at[s, yy * XC + cc], dst_ref=gath.at[s, y, xc],
                send_sem=p1_send.at[s], recv_sem=p1_recv.at[s],
                device_id=dev(z, cc, yy), device_id_type=MESH).start()

    def spread(s):
        pltpu.make_async_copy(gath.at[s], gath.at[s], p1_recv.at[s]).wait()
        total = gath[s, 0]
        for j in range(1, ny):
            total = total + gath[s, j]
        ring[s, z] = total
        for oz in far_first(nz):
            pltpu.make_async_remote_copy(
                src_ref=ring.at[s, z], dst_ref=ring.at[s, z],
                send_sem=ag_send.at[s], recv_sem=ag_recv.at[s],
                device_id=dev((z + oz) % nz, xc, y), device_id_type=MESH).start()

    w_in.wait()
    x_copy(0).wait()
    red[pl.ds(0, CHUNK), :] = jnp.dot(xv[pl.ds(0, CHUNK), :], wi[...], preferred_element_type=f32)

    pl.semaphore_wait(barrier, len(group) + nz - 1)
    idxc[xc] = idrow[...]
    for oc in far_first(XC):
        pltpu.make_async_remote_copy(
            src_ref=idrow, dst_ref=idxc.at[xc], send_sem=id_send, recv_sem=id_recv,
            device_id=dev(z, (xc + oc) % XC, y), device_id_type=MESH).start()

    w_out.wait()
    g_copy(0).wait()
    prj[pl.ds(0, CHUNK), :] = jnp.dot(gv[pl.ds(0, CHUNK), :], wo[...], preferred_element_type=f32)

    def step(i, _):
        project(i)
        return 0

    lax.fori_loop(1, chunks // 2, step, 0)
    s0, s1 = sketch(0, members(0))
    put(0, s0)
    scatter(0)

    pltpu.make_async_copy(idxc.at[pl.ds(0, XC - 1)], idxc.at[pl.ds(0, XC - 1)], id_recv).wait()
    ids = idxc[0]
    for j in range(1, XC):
        ids = ids + idxc[j]
    idz[z] = ids
    for oz in far_first(nz):
        pltpu.make_async_remote_copy(
            src_ref=idz.at[z], dst_ref=idz.at[z], send_sem=idz_send, recv_sem=idz_recv,
            device_id=dev((z + oz) % nz, xc, y), device_id_type=MESH).start()

    lax.fori_loop(chunks // 2, chunks, step, 0)
    put(1, s1 + sketch(1, members(1)[1:])[0])
    scatter(1)

    spread(0)
    pltpu.make_async_copy(idz.at[pl.ds(0, nz - 1)], idz.at[pl.ds(0, nz - 1)], idz_recv).wait()
    ids = idz[0]
    for j in range(1, nz):
        ids = ids + idz[j]
    for i in range(2 * XC):
        hit = jnp.where((ids == 2 * XC * z + i) & (lane < slots), lane, 0)
        where_smem[i] = jnp.max(hit)
    spread(1)

    for s in range(2):
        pltpu.make_async_copy(ring.at[s, pl.ds(0, nz - 1)], ring.at[s, pl.ds(0, nz - 1)], ag_recv.at[s]).wait()

    side, place = y // 2, (y % 2) * XC + xc
    for oc in far_first(XC) + [0]:
        cc = (xc + oc) % XC
        for p in range(2):
            yy = 2 * p + side
            src = where_smem[2 * cc + p]
            s, rest = src // (slots // 2), src % (slots // 2)
            pick[2 * cc + p] = ring[s, rest // XC, rest % XC]
            if oc == 0:
                @pl.when(yy == y)
                def _():
                    pltpu.make_async_copy(pick.at[2 * cc + p], out_ref.at[place], p3_recv).start()

                @pl.when(yy != y)
                def _():
                    pltpu.make_async_remote_copy(
                        src_ref=pick.at[2 * cc + p], dst_ref=out_ref.at[place],
                        send_sem=p3_send, recv_sem=p3_recv,
                        device_id=dev(z, cc, yy), device_id_type=MESH).start()
            else:
                pltpu.make_async_remote_copy(
                    src_ref=pick.at[2 * cc + p], dst_ref=out_ref.at[place],
                    send_sem=p3_send, recv_sem=p3_recv,
                    device_id=dev(z, cc, yy), device_id_type=MESH).start()

    def sent(ref, sem):
        pltpu.make_async_copy(ref, ref, sem).wait()

    sent(idxc.at[pl.ds(0, XC - 1)], id_send)
    sent(idz.at[pl.ds(0, nz - 1)], idz_send)
    for s in range(2):
        sent(part.at[s, pl.ds(0, npiece - 1)], p1_send.at[s])
        sent(ring.at[s, pl.ds(0, nz - 1)], ag_send.at[s])
    own = (y == side) | (y == 2 + side)

    @pl.when(own)
    def _():
        sent(pick.at[pl.ds(0, 2 * XC - 1)], p3_send)

    @pl.when(jnp.logical_not(own))
    def _():
        sent(pick, p3_send)

    pltpu.make_async_copy(out_ref, out_ref, p3_recv).wait()


def body(nz, ny, patches, hidden_grads, proj_in, proj_out, slot_image, patch_counts):
    rows, depth = patches.shape
    hidden = hidden_grads.shape[1]
    kw, lw = proj_in.shape[1], proj_out.shape[1]
    t = kw // (ny * XC)
    chunks = rows // CHUNK
    f32, i32, bf16 = jnp.float32, jnp.int32, jnp.bfloat16
    dma = pltpu.SemaphoreType.DMA
    out = pl.pallas_call(
        functools.partial(kernel, nz, ny),
        out_shape=jax.ShapeDtypeStruct((2 * XC, t, lw), f32),
        in_specs=[pl.BlockSpec(memory_space=pltpu.SMEM)] * 2 + [pl.BlockSpec(memory_space=pltpu.HBM)] * 4,
        out_specs=pl.BlockSpec(memory_space=pltpu.VMEM),
        scratch_shapes=[
            pltpu.VMEM((rows, depth), bf16), pltpu.VMEM((rows, hidden), bf16),
            pltpu.VMEM((depth, kw), bf16), pltpu.VMEM((hidden, lw), bf16),
            pltpu.VMEM((rows, kw), f32), pltpu.VMEM((rows, lw), f32),
            pltpu.VMEM((2, ny * XC, t, lw), f32),
            pltpu.VMEM((2, ny, XC, t, lw), f32),
            pltpu.VMEM((2, nz, XC, t, lw), f32),
            pltpu.VMEM((2 * XC, t, lw), f32),
            pltpu.VMEM((8, 128), i32), pltpu.VMEM((XC, 8, 128), i32), pltpu.VMEM((nz, 8, 128), i32),
            pltpu.SMEM((2 * XC,), i32),
            dma((chunks,)), dma((chunks,)), dma((2,)), dma, dma, dma, dma,
            dma((2,)), dma((2,)), dma((2,)), dma((2,)), dma, dma,
        ],
        name="sketch",
        compiler_params=pltpu.CompilerParams(collective_id=0, has_side_effects=True, vmem_limit_bytes=56 << 20),
    )(slot_image, patch_counts, patches, hidden_grads, proj_in, proj_out)
    return out.reshape(2 * XC * t, lw)


def solution(mesh):
    ny = mesh.shape["hid"]
    nz = mesh.shape["img"] // XC
    in_specs = (P("img", None), P("img", "hid"), P(), P("hid", None), P("img"), P("img"))
    return jax.shard_map(
        functools.partial(body, nz, ny), mesh=mesh, in_specs=in_specs,
        out_specs=P(("img", "hid"), None), check_vma=False)
```

```python
import functools

import jax
import jax.numpy as jnp
from jax import lax
from jax.experimental import pallas as pl
from jax.experimental.pallas import tpu as pltpu
from jax.sharding import PartitionSpec as P

MESH = pl.DeviceIdType.MESH
XC = 8
CUTS = 4
AHEAD = 3


def far_first(n):
    return sorted(range(1, n), key=lambda o: -min(o, n - o))


def middle_out(j, n):
    return n // 2 + lax.div(j + 1, 2) * (1 - 2 * lax.rem(j, 2))


def split(v):
    hi = v.astype(jnp.bfloat16)
    lo = (v - hi.astype(jnp.float32)).astype(jnp.bfloat16)
    return hi, lo


def kernel(nz, ny, image_ref, count_ref, x_hbm, g_hbm, wi_hbm, wo_hbm, out_ref,
           xv, gv, wi, wo, red, prj, later, part, gath, ring, pick, idrow, idxc, idz, where_smem,
           x_sem, g_sem, wi_sem, wo_sem, id_send, id_recv, idz_send, idz_recv,
           p1_send, p1_recv, ag_send, ag_recv, p3_send, p3_recv):
    b, y = lax.axis_index("img"), lax.axis_index("hid")
    z, xc = lax.div(b, XC), lax.rem(b, XC)
    rows, depth = xv.shape
    kw, lw = wi.shape[1], wo.shape[1]
    half_rows, cols = rows // 2, depth // CUTS
    npiece = ny * XC
    t = kw // npiece
    slots = 2 * nz * XC
    f32 = jnp.float32

    def at_z(o):
        return (lax.rem(z + o, nz) * XC + xc, y)

    def at_xc(o):
        return lax.rem(xc + o, XC)

    def row_part(h):
        return pl.ds(pl.multiple_of(h * half_rows, half_rows), half_rows)

    def col_part(q):
        return pl.ds(pl.multiple_of(q * cols, cols), cols)

    def rows_in(h, q):
        r, c = row_part(h), col_part(q)
        return (
            pltpu.make_async_copy(x_hbm.at[r, c], xv.at[r, c], x_sem.at[h, q]),
            pltpu.make_async_copy(g_hbm.at[r, c], gv.at[r, c], g_sem.at[h, q]),
        )

    def weights_in(q):
        c = col_part(q)
        return (
            pltpu.make_async_copy(wi_hbm.at[c], wi.at[c], wi_sem.at[q]),
            pltpu.make_async_copy(wo_hbm.at[c], wo.at[c], wo_sem.at[q]),
        )

    for q in range(AHEAD):
        (x_in, g_in), (a_in, o_in) = rows_in(0, q), weights_in(q)
        a_in.start()
        x_in.start()
        o_in.start()
        g_in.start()

    barrier = pltpu.get_barrier_semaphore()

    def greet(i, _):
        o = i + 1
        to = (z * XC + lax.rem(xc + lax.rem(o, XC), XC), lax.rem(y + lax.div(o, XC), ny))
        pl.semaphore_signal(barrier, inc=1, device_id=to, device_id_type=MESH)
        return 0

    lax.fori_loop(0, npiece - 1, greet, 0)
    for o in range(1, nz):
        pl.semaphore_signal(barrier, inc=1, device_id=at_z(o), device_id_type=MESH)

    lane = lax.broadcasted_iota(jnp.int32, (8, 128), 1)
    first, second = image_ref[0], image_ref[1]
    idrow[...] = jnp.where(lane == b, first, jnp.where(lane == slots // 2 + b, second, 0))
    c0, c1 = count_ref[0], count_ref[1]

    def sketch(a, h, start, count):
        pos = lax.broadcasted_iota(jnp.int32, (half_rows, lw), 0) + h * half_rows
        hi, lo = split(jnp.where((pos >= start) & (pos < start + count), prj[...], 0.0))
        full = jnp.dot(a, jnp.concatenate([hi, lo], axis=1), preferred_element_type=f32)
        return full[:kw, :lw] + (full[:kw, lw:] + full[kw:, :lw])

    def send_piece(s, cc, yy):
        pltpu.make_async_remote_copy(
            src_ref=part.at[s, yy * XC + cc], dst_ref=gath.at[s, y, xc],
            send_sem=p1_send.at[s], recv_sem=p1_recv.at[s, xc],
            device_id=(z * XC + cc, yy), device_id_type=MESH).start()

    later[...] = jnp.zeros_like(later)

    def half(h, _):
        def step(q, _):
            for c in rows_in(h, q):
                c.wait()

            @pl.when(h == 0)
            def _():
                for c in weights_in(q):
                    c.wait()

            n = h * CUTS + q + AHEAD

            @pl.when(n < 2 * CUTS)
            def _():
                hh, qq = lax.div(n, CUTS), lax.rem(n, CUTS)

                @pl.when(hh == 0)
                def _():
                    for c in weights_in(qq):
                        c.start()

                for c in rows_in(hh, qq):
                    c.start()

            @pl.when(q == 0)
            def _():
                red[...] = jnp.zeros_like(red)
                prj[...] = jnp.zeros_like(prj)

            r, c = row_part(h), col_part(q)
            red[...] += jnp.dot(xv[r, c], wi[c, :], preferred_element_type=f32)
            prj[...] += jnp.dot(gv[r, c], wo[c, :], preferred_element_type=f32)
            return 0

        lax.fori_loop(0, CUTS, step, 0)
        a = jnp.concatenate(split(red[...].T), axis=0)
        value = later[...] + sketch(a, h, jnp.where(h == 0, 0, c0), jnp.where(h == 0, c0, c1))
        for i in range(npiece):
            part[h, i] = value[i * t : (i + 1) * t]

        @pl.when(h == 0)
        def _():
            pl.semaphore_wait(barrier, npiece + nz - 2)

        def to_row(j, _):
            yy = lax.rem(y + middle_out(j, ny), ny)
            for o in far_first(XC):
                send_piece(h, at_xc(o), yy)

            @pl.when(yy != y)
            def _():
                send_piece(h, xc, yy)

            return 0

        lax.fori_loop(0, ny, to_row, 0)
        pltpu.make_async_copy(part.at[h, y * XC + xc], gath.at[h, y, xc], p1_recv.at[h, xc]).start()

        @pl.when(h == 0)
        def _():
            for o in far_first(XC):
                pltpu.make_async_remote_copy(
                    src_ref=idrow, dst_ref=idxc.at[xc], send_sem=id_send, recv_sem=id_recv,
                    device_id=(z * XC + at_xc(o), y), device_id_type=MESH).start()
            idxc[xc] = idrow[...]
            later[...] = sketch(a, 0, c0, c1)

        return 0

    lax.fori_loop(0, 2, half, 0)

    def spread(s):
        def one(j, _):
            src = at_xc(XC - middle_out(XC - 1 - j, XC))
            pltpu.make_async_copy(gath.at[s, :, 0], gath.at[s, :, 0], p1_recv.at[s, src]).wait()
            total = gath[s, 0, src]
            for i in range(1, ny):
                total = total + gath[s, i, src]
            ring[s, z, src] = total
            for o in far_first(nz):
                pltpu.make_async_remote_copy(
                    src_ref=ring.at[s, z, src], dst_ref=ring.at[s, z, src],
                    send_sem=ag_send.at[s], recv_sem=ag_recv.at[s],
                    device_id=at_z(o), device_id_type=MESH).start()
            return 0

        lax.fori_loop(0, XC, one, 0)

    def add_ids(s, _):
        @pl.when(s == 1)
        def _():
            pltpu.make_async_copy(idxc.at[pl.ds(0, XC - 1)], idxc.at[pl.ds(0, XC - 1)], id_recv).wait()
            ids = idxc[0]
            for j in range(1, XC):
                ids = ids + idxc[j]
            idz[z] = ids
            for o in far_first(nz):
                pltpu.make_async_remote_copy(
                    src_ref=idz.at[z], dst_ref=idz.at[z], send_sem=idz_send, recv_sem=idz_recv,
                    device_id=at_z(o), device_id_type=MESH).start()

        spread(s)
        return 0

    lax.fori_loop(0, 2, add_ids, 0)

    pltpu.make_async_copy(idz.at[pl.ds(0, nz - 1)], idz.at[pl.ds(0, nz - 1)], idz_recv).wait()
    ids = idz[0]
    for j in range(1, nz):
        ids = ids + idz[j]
    for i in range(2 * XC):
        where_smem[i] = jnp.max(jnp.where((ids == 2 * XC * z + i) & (lane < slots), lane, 0))

    def sent(ref, sem):
        pltpu.make_async_copy(ref, ref, sem).wait()

    sent(idxc.at[pl.ds(0, XC - 1)], id_send)
    sent(idz.at[pl.ds(0, nz - 1)], idz_send)
    for s in range(2):
        sent(part.at[s, pl.ds(0, npiece - 1)], p1_send.at[s])
    for s in range(2):
        pltpu.make_async_copy(ring.at[s, pl.ds(0, nz - 1)], ring.at[s, pl.ds(0, nz - 1)], ag_recv.at[s]).wait()

    side = lax.div(y, 2)
    place = lax.rem(y, 2) * XC + xc

    def take(i):
        src = where_smem[i]
        pick[i] = ring[lax.div(src, slots // 2), lax.rem(lax.div(src, XC), nz), lax.rem(src, XC)]

    def deliver(i, cc, yy):
        pltpu.make_async_remote_copy(
            src_ref=pick.at[i], dst_ref=out_ref.at[place], send_sem=p3_send, recv_sem=p3_recv,
            device_id=(z * XC + cc, yy), device_id_type=MESH).start()

    def to_owner(j, _):
        cc = at_xc(middle_out(j, XC))
        for p in range(2):
            take(2 * cc + p)
            deliver(2 * cc + p, cc, 2 * p + side)
        return 0

    lax.fori_loop(0, XC - 1, to_owner, 0)
    for p in range(2):
        yy = 2 * p + side
        take(2 * xc + p)

        @pl.when(yy == y)
        def _():
            pltpu.make_async_copy(pick.at[2 * xc + p], out_ref.at[place], p3_recv).start()

        @pl.when(yy != y)
        def _():
            deliver(2 * xc + p, xc, yy)

    for s in range(2):
        sent(ring.at[s, pl.ds(0, nz - 1)], ag_send.at[s])
    own = (y == side) | (y == 2 + side)

    @pl.when(own)
    def _():
        sent(pick.at[pl.ds(0, 2 * XC - 1)], p3_send)

    @pl.when(jnp.logical_not(own))
    def _():
        sent(pick, p3_send)

    pltpu.make_async_copy(out_ref, out_ref, p3_recv).wait()


def body(nz, ny, patches, hidden_grads, proj_in, proj_out, slot_image, patch_counts):
    rows, depth = patches.shape
    hidden = hidden_grads.shape[1]
    kw, lw = proj_in.shape[1], proj_out.shape[1]
    t = kw // (ny * XC)
    f32, i32, bf16 = jnp.float32, jnp.int32, jnp.bfloat16
    dma = pltpu.SemaphoreType.DMA
    out = pl.pallas_call(
        functools.partial(kernel, nz, ny),
        out_shape=jax.ShapeDtypeStruct((2 * XC, t, lw), f32),
        in_specs=[pl.BlockSpec(memory_space=pltpu.SMEM)] * 2 + [pl.BlockSpec(memory_space=pltpu.HBM)] * 4,
        out_specs=pl.BlockSpec(memory_space=pltpu.HBM),
        scratch_shapes=[
            pltpu.VMEM((rows, depth), bf16), pltpu.VMEM((rows, hidden), bf16),
            pltpu.VMEM((depth, kw), bf16), pltpu.VMEM((hidden, lw), bf16),
            pltpu.VMEM((rows // 2, kw), f32), pltpu.VMEM((rows // 2, lw), f32), pltpu.VMEM((kw, lw), f32),
            pltpu.VMEM((2, ny * XC, t, lw), f32),
            pltpu.VMEM((2, ny, XC, t, lw), f32),
            pltpu.VMEM((2, nz, XC, t, lw), f32),
            pltpu.VMEM((2 * XC, t, lw), f32),
            pltpu.VMEM((8, 128), i32), pltpu.VMEM((XC, 8, 128), i32), pltpu.VMEM((nz, 8, 128), i32),
            pltpu.SMEM((2 * XC,), i32),
            dma((2, CUTS)), dma((2, CUTS)), dma((CUTS,)), dma((CUTS,)), dma, dma, dma, dma,
            dma((2,)), dma((2, XC)), dma((2,)), dma((2,)), dma, dma,
        ],
        name="sketch",
        compiler_params=pltpu.CompilerParams(collective_id=0, has_side_effects=True, vmem_limit_bytes=56 << 20),
    )(slot_image, patch_counts, patches, hidden_grads, proj_in, proj_out)
    return out.reshape(2 * XC * t, lw)


def solution(mesh):
    ny = mesh.shape["hid"]
    nz = mesh.shape["img"] // XC
    in_specs = (P("img", None), P("img", "hid"), P(), P("hid", None), P("img"), P("img"))
    return jax.shard_map(
        functools.partial(body, nz, ny), mesh=mesh, in_specs=in_specs,
        out_specs=P(("img", "hid"), None), check_vma=False)
```

```python
import functools

import jax
import jax.numpy as jnp
from jax import lax
from jax.experimental import pallas as pl
from jax.experimental.pallas import tpu as pltpu
from jax.sharding import PartitionSpec as P

MESH = pl.DeviceIdType.MESH
XC = 8
NEAR = 2
CUTS = 4
AHEAD = 3


def far_first(n):
    return sorted(range(1, n), key=lambda o: -min(o, n - o))


def middle_out(j, n):
    return n // 2 + lax.div(j + 1, 2) * (1 - 2 * lax.rem(j, 2))


def split(v):
    hi = v.astype(jnp.bfloat16)
    lo = (v - hi.astype(jnp.float32)).astype(jnp.bfloat16)
    return hi, lo


def kernel(nz, ny, image_ref, count_ref, x_hbm, g_hbm, wi_hbm, wo_hbm, out_ref,
           xv, gv, wi, wo, red, prj, later, part, gath, ring, pick, idrow, idxc, idz, where_smem,
           x_sem, g_sem, wi_sem, wo_sem, id_send, id_recv, idz_send, idz_recv,
           p1_send, p1_recv, ag_send, ag_recv, p3_send, p3_recv):
    b, y = lax.axis_index("img"), lax.axis_index("hid")
    z, xc = lax.div(b, XC), lax.rem(b, XC)
    rows, depth = xv.shape
    kw, lw = wi.shape[1], wo.shape[1]
    half_rows, cols = rows // 2, depth // CUTS
    npiece = ny * NEAR
    block, here = lax.div(xc, NEAR), lax.rem(xc, NEAR)
    t = kw // npiece
    slots = 2 * nz * XC
    f32 = jnp.float32

    def at_z(o):
        return (lax.rem(z + o, nz) * XC + xc, y)

    def at_xc(o):
        return lax.rem(xc + o, XC)

    def near(o):
        return lax.rem(here + o, NEAR)

    def to_near(k):
        return z * XC + block * NEAR + k

    def row_part(h):
        return pl.ds(pl.multiple_of(h * half_rows, half_rows), half_rows)

    def col_part(q):
        return pl.ds(pl.multiple_of(q * cols, cols), cols)

    def rows_in(h, q):
        r, c = row_part(h), col_part(q)
        return (
            pltpu.make_async_copy(x_hbm.at[r, c], xv.at[r, c], x_sem.at[h, q]),
            pltpu.make_async_copy(g_hbm.at[r, c], gv.at[r, c], g_sem.at[h, q]),
        )

    def weights_in(q):
        c = col_part(q)
        return (
            pltpu.make_async_copy(wi_hbm.at[c], wi.at[c], wi_sem.at[q]),
            pltpu.make_async_copy(wo_hbm.at[c], wo.at[c], wo_sem.at[q]),
        )

    for q in range(AHEAD):
        (x_in, g_in), (a_in, o_in) = rows_in(0, q), weights_in(q)
        a_in.start()
        x_in.start()
        o_in.start()
        g_in.start()

    barrier = pltpu.get_barrier_semaphore()

    def greet(i, _):
        o = i + 1
        to = (z * XC + lax.rem(xc + lax.rem(o, XC), XC), lax.rem(y + lax.div(o, XC), ny))
        pl.semaphore_signal(barrier, inc=1, device_id=to, device_id_type=MESH)
        return 0

    lax.fori_loop(0, ny * XC - 1, greet, 0)
    for o in range(1, nz):
        pl.semaphore_signal(barrier, inc=1, device_id=at_z(o), device_id_type=MESH)

    lane = lax.broadcasted_iota(jnp.int32, (8, 128), 1)
    first, second = image_ref[0], image_ref[1]
    idrow[...] = jnp.where(lane == b, first + 1, jnp.where(lane == slots // 2 + b, second + 1, 0))
    c0, c1 = count_ref[0], count_ref[1]

    def sketch(a, h, start, count):
        pos = lax.broadcasted_iota(jnp.int32, (half_rows, lw), 0) + h * half_rows
        hi, lo = split(jnp.where((pos >= start) & (pos < start + count), prj[...], 0.0))
        full = jnp.dot(a, jnp.concatenate([hi, lo], axis=1), preferred_element_type=f32)
        return full[:kw, :lw] + (full[:kw, lw:] + full[kw:, :lw])

    def send_piece(s, k, yy):
        pltpu.make_async_remote_copy(
            src_ref=part.at[s, yy * NEAR + k], dst_ref=gath.at[s, y, here],
            send_sem=p1_send.at[s], recv_sem=p1_recv.at[s, here],
            device_id=(to_near(k), yy), device_id_type=MESH).start()

    later[...] = jnp.zeros_like(later)

    def half(h, _):
        def step(q, _):
            for c in rows_in(h, q):
                c.wait()

            @pl.when(h == 0)
            def _():
                for c in weights_in(q):
                    c.wait()

            n = h * CUTS + q + AHEAD

            @pl.when(n < 2 * CUTS)
            def _():
                hh, qq = lax.div(n, CUTS), lax.rem(n, CUTS)

                @pl.when(hh == 0)
                def _():
                    for c in weights_in(qq):
                        c.start()

                for c in rows_in(hh, qq):
                    c.start()

            @pl.when(q == 0)
            def _():
                red[...] = jnp.zeros_like(red)
                prj[...] = jnp.zeros_like(prj)

            r, c = row_part(h), col_part(q)
            red[...] += jnp.dot(xv[r, c], wi[c, :], preferred_element_type=f32)
            prj[...] += jnp.dot(gv[r, c], wo[c, :], preferred_element_type=f32)
            return 0

        lax.fori_loop(0, CUTS, step, 0)
        a = jnp.concatenate(split(red[...].T), axis=0)
        value = later[...] + sketch(a, h, jnp.where(h == 0, 0, c0), jnp.where(h == 0, c0, c1))
        for i in range(npiece):
            part[h, i] = value[i * t : (i + 1) * t]

        @pl.when(h == 0)
        def _():
            pl.semaphore_wait(barrier, ny * XC + nz - 2)

        def to_row(j, _):
            yy = lax.rem(y + middle_out(j, ny), ny)
            for o in far_first(NEAR):
                send_piece(h, near(o), yy)

            @pl.when(yy != y)
            def _():
                send_piece(h, here, yy)

            return 0

        lax.fori_loop(0, ny, to_row, 0)
        pltpu.make_async_copy(part.at[h, y * NEAR + here], gath.at[h, y, here], p1_recv.at[h, here]).start()

        @pl.when(h == 0)
        def _():
            for o in far_first(NEAR):
                pltpu.make_async_remote_copy(
                    src_ref=idrow, dst_ref=idxc.at[here], send_sem=id_send, recv_sem=id_recv,
                    device_id=(to_near(near(o)), y), device_id_type=MESH).start()
            idxc[here] = idrow[...]
            later[...] = sketch(a, 0, c0, c1)

        return 0

    lax.fori_loop(0, 2, half, 0)

    def spread(s):
        def one(j, _):
            src = near(NEAR - middle_out(NEAR - 1 - j, NEAR))
            pltpu.make_async_copy(gath.at[s, :, 0], gath.at[s, :, 0], p1_recv.at[s, src]).wait()
            total = gath[s, 0, src]
            for i in range(1, ny):
                total = total + gath[s, i, src]
            ring[s, z, src] = total
            for o in far_first(nz):
                pltpu.make_async_remote_copy(
                    src_ref=ring.at[s, z, src], dst_ref=ring.at[s, z, src],
                    send_sem=ag_send.at[s], recv_sem=ag_recv.at[s],
                    device_id=at_z(o), device_id_type=MESH).start()
            return 0

        lax.fori_loop(0, NEAR, one, 0)

    def add_ids(s, _):
        @pl.when(s == 1)
        def _():
            pltpu.make_async_copy(idxc.at[pl.ds(0, NEAR - 1)], idxc.at[pl.ds(0, NEAR - 1)], id_recv).wait()
            ids = idxc[0]
            for j in range(1, NEAR):
                ids = ids + idxc[j]
            idz[z] = ids
            for o in far_first(nz):
                pltpu.make_async_remote_copy(
                    src_ref=idz.at[z], dst_ref=idz.at[z], send_sem=idz_send, recv_sem=idz_recv,
                    device_id=at_z(o), device_id_type=MESH).start()

        spread(s)
        return 0

    lax.fori_loop(0, 2, add_ids, 0)

    pltpu.make_async_copy(idz.at[pl.ds(0, nz - 1)], idz.at[pl.ds(0, nz - 1)], idz_recv).wait()
    ids = idz[0]
    for j in range(1, nz):
        ids = ids + idz[j]
    for i in range(2 * XC):
        where_smem[i] = jnp.max(jnp.where(ids == 2 * XC * z + i + 1, lane, -1))

    def sent(ref, sem):
        pltpu.make_async_copy(ref, ref, sem).wait()

    sent(idxc.at[pl.ds(0, NEAR - 1)], id_send)
    sent(idz.at[pl.ds(0, nz - 1)], idz_send)
    for s in range(2):
        sent(part.at[s, pl.ds(0, npiece - 1)], p1_send.at[s])
    for s in range(2):
        pltpu.make_async_copy(ring.at[s, pl.ds(0, nz - 1)], ring.at[s, pl.ds(0, nz - 1)], ag_recv.at[s]).wait()

    side = lax.div(y, 2)
    place = lax.rem(y, 2) * NEAR + here

    def take(i):
        found = where_smem[i]
        src = jnp.maximum(found, 0)
        piece = ring[lax.div(src, slots // 2), lax.rem(lax.div(src, XC), nz), lax.rem(src, NEAR)]
        pick[i] = jnp.where(found >= 0, piece, 0.0)

    def deliver(i, cc, yy):
        pltpu.make_async_remote_copy(
            src_ref=pick.at[i], dst_ref=out_ref.at[block, place], send_sem=p3_send, recv_sem=p3_recv,
            device_id=(z * XC + cc, yy), device_id_type=MESH).start()

    def to_owner(j, _):
        cc = at_xc(middle_out(j, XC))
        for p in range(2):
            take(2 * cc + p)
            deliver(2 * cc + p, cc, 2 * p + side)
        return 0

    lax.fori_loop(0, XC - 1, to_owner, 0)
    for p in range(2):
        yy = 2 * p + side
        take(2 * xc + p)

        @pl.when(yy == y)
        def _():
            pltpu.make_async_copy(pick.at[2 * xc + p], out_ref.at[block, place], p3_recv).start()

        @pl.when(yy != y)
        def _():
            deliver(2 * xc + p, xc, yy)

    for s in range(2):
        sent(ring.at[s, pl.ds(0, nz - 1)], ag_send.at[s])
    own = (y == side) | (y == 2 + side)

    @pl.when(own)
    def _():
        sent(pick.at[pl.ds(0, 2 * XC - 1)], p3_send)

    @pl.when(jnp.logical_not(own))
    def _():
        sent(pick, p3_send)

    pltpu.make_async_copy(out_ref, out_ref, p3_recv).wait()


def body(nz, ny, patches, hidden_grads, proj_in, proj_out, slot_image, patch_counts):
    rows, depth = patches.shape
    hidden = hidden_grads.shape[1]
    kw, lw = proj_in.shape[1], proj_out.shape[1]
    t = kw // (ny * NEAR)
    f32, i32, bf16 = jnp.float32, jnp.int32, jnp.bfloat16
    dma = pltpu.SemaphoreType.DMA
    out = pl.pallas_call(
        functools.partial(kernel, nz, ny),
        out_shape=pltpu.VMEM((XC // NEAR, 2 * NEAR, t, lw), f32),
        in_specs=[pl.BlockSpec(memory_space=pltpu.SMEM)] * 2 + [pl.BlockSpec(memory_space=pltpu.HBM)] * 4,
        out_specs=pl.BlockSpec(memory_space=pltpu.VMEM),
        scratch_shapes=[
            pltpu.VMEM((rows, depth), bf16), pltpu.VMEM((rows, hidden), bf16),
            pltpu.VMEM((depth, kw), bf16), pltpu.VMEM((hidden, lw), bf16),
            pltpu.VMEM((rows // 2, kw), f32), pltpu.VMEM((rows // 2, lw), f32), pltpu.VMEM((kw, lw), f32),
            pltpu.VMEM((2, ny * NEAR, t, lw), f32),
            pltpu.VMEM((2, ny, NEAR, t, lw), f32),
            pltpu.VMEM((2, nz, NEAR, t, lw), f32),
            pltpu.VMEM((2 * XC, t, lw), f32),
            pltpu.VMEM((8, 128), i32), pltpu.VMEM((NEAR, 8, 128), i32), pltpu.VMEM((nz, 8, 128), i32),
            pltpu.SMEM((2 * XC,), i32),
            dma((2, CUTS)), dma((2, CUTS)), dma((CUTS,)), dma((CUTS,)), dma, dma, dma, dma,
            dma((2,)), dma((2, NEAR)), dma((2,)), dma((2,)), dma, dma,
        ],
        name="sketch",
        compiler_params=pltpu.CompilerParams(collective_id=0, has_side_effects=True, vmem_limit_bytes=56 << 20),
    )(slot_image, patch_counts, patches, hidden_grads, proj_in, proj_out)
    return out.reshape(XC // NEAR, 2 * NEAR * t, lw).sum(0)


def solution(mesh):
    ny = mesh.shape["hid"]
    nz = mesh.shape["img"] // XC
    in_specs = (P("img", None), P("img", "hid"), P(), P("hid", None), P("img"), P("img"))
    return jax.shard_map(
        functools.partial(body, nz, ny), mesh=mesh, in_specs=in_specs,
        out_specs=P(("img", "hid"), None), check_vma=False)
```

```python
import functools

import jax
import jax.numpy as jnp
from jax import lax
from jax.experimental import pallas as pl
from jax.experimental.pallas import tpu as pltpu
from jax.sharding import PartitionSpec as P

MESH = pl.DeviceIdType.MESH
XC = 8
NEAR = 2
CUTS = 3
AHEAD = 3


def far_first(n):
    return sorted(range(1, n), key=lambda o: -min(o, n - o))


def middle_out(j, n):
    return n // 2 + lax.div(j + 1, 2) * (1 - 2 * lax.rem(j, 2))


def split(v):
    hi = v.astype(jnp.bfloat16)
    lo = (v - hi.astype(jnp.float32)).astype(jnp.bfloat16)
    return hi, lo


def kernel(nz, ny, image_hbm, count_hbm, x_hbm, g_hbm, wi_hbm, wo_hbm, out_ref,
           xv, gv, wi, wo, red, prj, later, part, gath, ring, pick, idrow, idxc, idz, where_smem, image_ref, count_ref,
           image_sem, count_sem, x_sem, g_sem, wi_sem, wo_sem, id_send, id_recv, idz_send, idz_recv,
           p1_send, p1_recv, ag_send, ag_recv, p3_send, p3_recv):
    b, y = lax.axis_index("img"), lax.axis_index("hid")
    z, xc = lax.div(b, XC), lax.rem(b, XC)
    rows, depth = xv.shape
    kw, lw = wi.shape[1], wo.shape[1]
    half_rows, cols = rows // 2, depth // CUTS
    npiece = ny * NEAR
    block, here = lax.div(xc, NEAR), lax.rem(xc, NEAR)
    t = kw // npiece
    slots = 2 * nz * XC
    f32 = jnp.float32

    def at_z(o):
        return (lax.rem(z + o, nz) * XC + xc, y)

    def at_xc(o):
        return lax.rem(xc + o, XC)

    def near(o):
        return lax.rem(here + o, NEAR)

    def to_near(k):
        return z * XC + block * NEAR + k

    def row_part(h):
        return pl.ds(pl.multiple_of(h * half_rows, half_rows), half_rows)

    def col_part(q):
        return pl.ds(pl.multiple_of(q * cols, cols), cols)

    def rows_in(h, q):
        r, c = row_part(h), col_part(q)
        return (
            pltpu.make_async_copy(x_hbm.at[r, c], xv.at[r, c], x_sem.at[h, q]),
            pltpu.make_async_copy(g_hbm.at[r, c], gv.at[r, c], g_sem.at[h, q]),
        )

    def weights_in(q):
        c = col_part(q)
        return (
            pltpu.make_async_copy(wi_hbm.at[c], wi.at[c], wi_sem.at[q]),
            pltpu.make_async_copy(wo_hbm.at[c], wo.at[c], wo_sem.at[q]),
        )

    for q in range(AHEAD):
        (x_in, g_in), (a_in, o_in) = rows_in(0, q), weights_in(q)
        a_in.start()
        x_in.start()
        o_in.start()
        g_in.start()

    image_in = pltpu.make_async_copy(image_hbm, image_ref, image_sem)
    count_in = pltpu.make_async_copy(count_hbm, count_ref, count_sem)
    image_in.start()
    count_in.start()

    barrier = pltpu.get_barrier_semaphore()

    def greet(i, _):
        o = i + 1
        to = (z * XC + lax.rem(xc + lax.rem(o, XC), XC), lax.rem(y + lax.div(o, XC), ny))
        pl.semaphore_signal(barrier, inc=1, device_id=to, device_id_type=MESH)
        return 0

    lax.fori_loop(0, ny * XC - 1, greet, 0)
    for o in range(1, nz):
        pl.semaphore_signal(barrier, inc=1, device_id=at_z(o), device_id_type=MESH)

    later[...] = jnp.zeros_like(later)

    image_in.wait()
    count_in.wait()
    lane = lax.broadcasted_iota(jnp.int32, (8, 128), 1)
    first, second = image_ref[0], image_ref[1]
    idrow[...] = jnp.where(lane == b, first + 1, jnp.where(lane == slots // 2 + b, second + 1, 0))
    c0, c1 = count_ref[0], count_ref[1]

    def sketch(a, h, start, count):
        pos = lax.broadcasted_iota(jnp.int32, (half_rows, lw), 0) + h * half_rows
        hi, lo = split(jnp.where((pos >= start) & (pos < start + count), prj[...], 0.0))
        full = jnp.dot(a, jnp.concatenate([hi, lo], axis=1), preferred_element_type=f32)
        return full[:kw, :lw] + (full[:kw, lw:] + full[kw:, :lw])

    def side_of(yy):
        return lax.div(yy, 2)

    def quarter(yy):
        return yy

    def send_piece(s, k, yy):
        pltpu.make_async_remote_copy(
            src_ref=part.at[s, quarter(yy) * NEAR + k], dst_ref=gath.at[s, y, here],
            send_sem=p1_send.at[s], recv_sem=p1_recv.at[s, here],
            device_id=(to_near(k), yy), device_id_type=MESH).start()

    def half(h, _):
        def step(q, _):
            for c in rows_in(h, q):
                c.wait()

            @pl.when(h == 0)
            def _():
                for c in weights_in(q):
                    c.wait()

            n = h * CUTS + q + AHEAD

            @pl.when(n < 2 * CUTS)
            def _():
                hh, qq = lax.div(n, CUTS), lax.rem(n, CUTS)

                @pl.when(hh == 0)
                def _():
                    for c in weights_in(qq):
                        c.start()

                for c in rows_in(hh, qq):
                    c.start()

            @pl.when(q == 0)
            def _():
                red[...] = jnp.zeros_like(red)
                prj[...] = jnp.zeros_like(prj)

            r, c = row_part(h), col_part(q)
            red[...] += jnp.dot(xv[r, c], wi[c, :], preferred_element_type=f32)
            prj[...] += jnp.dot(gv[r, c], wo[c, :], preferred_element_type=f32)
            return 0

        lax.fori_loop(0, CUTS, step, 0)
        a = jnp.concatenate(split(red[...].T), axis=0)
        value = later[...] + sketch(a, h, jnp.where(h == 0, 0, c0), jnp.where(h == 0, c0, c1))
        for i in range(npiece):
            part[h, i] = value[i * t : (i + 1) * t]

        @pl.when(h == 0)
        def _():
            pl.semaphore_wait(barrier, ny * XC + nz - 2)

        def to_row(yy, _):
            for o in far_first(NEAR):
                send_piece(h, near(o), yy)

            @pl.when(yy != y)
            def _():
                send_piece(h, here, yy)

            return 0

        lax.fori_loop(0, ny, to_row, 0)
        pltpu.make_async_copy(part.at[h, quarter(y) * NEAR + here], gath.at[h, y, here], p1_recv.at[h, here]).start()

        @pl.when(h == 0)
        def _():
            for o in far_first(NEAR):
                pltpu.make_async_remote_copy(
                    src_ref=idrow, dst_ref=idxc.at[here], send_sem=id_send, recv_sem=id_recv,
                    device_id=(to_near(near(o)), y), device_id_type=MESH).start()
            idxc[here] = idrow[...]
            later[...] = sketch(a, 0, c0, c1)

        return 0

    lax.fori_loop(0, 2, half, 0)

    def others_z(j):
        return j + jnp.where(j >= z, 1, 0)

    def spread(s):
        for k in range(NEAR):
            pltpu.make_async_copy(gath.at[s, :, 0], gath.at[s, :, 0], p1_recv.at[s, k]).wait()
        total = gath[s, 0]
        for i in range(1, ny):
            total = total + gath[s, i]
        ring[s, z] = total

        def to_z(j, _):
            pltpu.make_async_remote_copy(
                src_ref=ring.at[s, z], dst_ref=ring.at[s, z],
                send_sem=ag_send.at[s], recv_sem=ag_recv.at[s],
                device_id=(others_z(j) * XC + xc, y), device_id_type=MESH).start()
            return 0

        lax.fori_loop(0, nz - 1, to_z, 0)

    def add_ids(s, _):
        @pl.when(s == 1)
        def _():
            pltpu.make_async_copy(idxc.at[pl.ds(0, NEAR - 1)], idxc.at[pl.ds(0, NEAR - 1)], id_recv).wait()
            ids = idxc[0]
            for j in range(1, NEAR):
                ids = ids + idxc[j]
            idz[z] = ids
            for o in far_first(nz):
                pltpu.make_async_remote_copy(
                    src_ref=idz.at[z], dst_ref=idz.at[z], send_sem=idz_send, recv_sem=idz_recv,
                    device_id=at_z(o), device_id_type=MESH).start()

        spread(s)
        return 0

    lax.fori_loop(0, 2, add_ids, 0)

    pltpu.make_async_copy(idz.at[pl.ds(0, nz - 1)], idz.at[pl.ds(0, nz - 1)], idz_recv).wait()
    ids = idz[0]
    for j in range(1, nz):
        ids = ids + idz[j]
    for i in range(2 * XC):
        where_smem[i] = jnp.max(jnp.where(ids == 2 * XC * z + i + 1, lane, -1))

    def sent(ref, sem):
        pltpu.make_async_copy(ref, ref, sem).wait()

    sent(idxc.at[pl.ds(0, NEAR - 1)], id_send)
    sent(idz.at[pl.ds(0, nz - 1)], idz_send)
    for s in range(2):
        sent(part.at[s, pl.ds(0, npiece - 1)], p1_send.at[s])
    for s in range(2):
        pltpu.make_async_copy(ring.at[s, pl.ds(0, nz - 1)], ring.at[s, pl.ds(0, nz - 1)], ag_recv.at[s]).wait()

    side = side_of(y)
    place = lax.rem(y, 2) * NEAR + here

    def take(i):
        found = where_smem[i]
        src = jnp.maximum(found, 0)
        piece = ring[lax.div(src, slots // 2), lax.rem(lax.div(src, XC), nz), lax.rem(src, NEAR)]
        pick[i] = jnp.where(found >= 0, piece, 0.0)

    def deliver(i, cc, yy):
        pltpu.make_async_remote_copy(
            src_ref=pick.at[i], dst_ref=out_ref.at[block, place], send_sem=p3_send, recv_sem=p3_recv,
            device_id=(z * XC + cc, yy), device_id_type=MESH).start()

    def to_owner(cc, _):
        for p in range(2):
            i, yy = 2 * cc + p, 2 * p + side
            take(i)

            @pl.when((cc == xc) & (yy == y))
            def _():
                pltpu.make_async_copy(pick.at[i], out_ref.at[block, place], p3_recv).start()

            @pl.when((cc != xc) | (yy != y))
            def _():
                deliver(i, cc, yy)

        return 0

    lax.fori_loop(0, XC, to_owner, 0)
    for s in range(2):
        sent(ring.at[s, pl.ds(0, nz - 1)], ag_send.at[s])
    own = (y == side) | (y == 2 + side)

    @pl.when(own)
    def _():
        sent(pick.at[pl.ds(0, 2 * XC - 1)], p3_send)

    @pl.when(jnp.logical_not(own))
    def _():
        sent(pick, p3_send)

    pltpu.make_async_copy(out_ref, out_ref, p3_recv).wait()


def body(nz, ny, patches, hidden_grads, proj_in, proj_out, slot_image, patch_counts):
    rows, depth = patches.shape
    hidden = hidden_grads.shape[1]
    kw, lw = proj_in.shape[1], proj_out.shape[1]
    t = kw // (ny * NEAR)
    f32, i32, bf16 = jnp.float32, jnp.int32, jnp.bfloat16
    dma = pltpu.SemaphoreType.DMA
    out = pl.pallas_call(
        functools.partial(kernel, nz, ny),
        out_shape=pltpu.VMEM((XC // NEAR, 2 * NEAR, t, lw), f32),
        in_specs=[pl.BlockSpec(memory_space=pltpu.HBM)] * 6,
        out_specs=pl.BlockSpec(memory_space=pltpu.VMEM),
        scratch_shapes=[
            pltpu.VMEM((rows, depth), bf16), pltpu.VMEM((rows, hidden), bf16),
            pltpu.VMEM((depth, kw), bf16), pltpu.VMEM((hidden, lw), bf16),
            pltpu.VMEM((rows // 2, kw), f32), pltpu.VMEM((rows // 2, lw), f32), pltpu.VMEM((kw, lw), f32),
            pltpu.VMEM((2, ny * NEAR, t, lw), f32),
            pltpu.VMEM((2, ny, NEAR, t, lw), f32),
            pltpu.VMEM((2, nz, NEAR, t, lw), f32),
            pltpu.VMEM((2 * XC, t, lw), f32),
            pltpu.VMEM((8, 128), i32), pltpu.VMEM((NEAR, 8, 128), i32), pltpu.VMEM((nz, 8, 128), i32),
            pltpu.SMEM((2 * XC,), i32), pltpu.SMEM((2,), i32), pltpu.SMEM((2,), i32), dma, dma,
            dma((2, CUTS)), dma((2, CUTS)), dma((CUTS,)), dma((CUTS,)), dma, dma, dma, dma,
            dma((2,)), dma((2, NEAR)), dma((2,)), dma((2,)), dma, dma,
        ],
        name="sketch",
        compiler_params=pltpu.CompilerParams(collective_id=0, has_side_effects=True, vmem_limit_bytes=56 << 20),
    )(slot_image, patch_counts, patches, hidden_grads, proj_in, proj_out)
    return out.reshape(XC // NEAR, 2 * NEAR * t, lw).sum(0)


def solution(mesh):
    ny = mesh.shape["hid"]
    nz = mesh.shape["img"] // XC
    in_specs = (P("img", None), P("img", "hid"), P(), P("hid", None), P("img"), P("img"))
    return jax.shard_map(
        functools.partial(body, nz, ny), mesh=mesh, in_specs=in_specs,
        out_specs=P(("img", "hid"), None), check_vma=False)
```

```python
import functools

import jax
import jax.numpy as jnp
from jax import lax
from jax.experimental import pallas as pl
from jax.experimental.pallas import tpu as pltpu
from jax.sharding import PartitionSpec as P

MESH = pl.DeviceIdType.MESH
XC = 8
NEAR = 2
CUTS = 3
AHEAD = 3


def far_first(n):
    return sorted(range(1, n), key=lambda o: -min(o, n - o))


def middle_out(j, n):
    return n // 2 + lax.div(j + 1, 2) * (1 - 2 * lax.rem(j, 2))


def split(v):
    hi = v.astype(jnp.bfloat16)
    lo = (v - hi.astype(jnp.float32)).astype(jnp.bfloat16)
    return hi, lo


def kernel(nz, ny, image_hbm, count_hbm, x_hbm, g_hbm, wi_hbm, wo_hbm, out_ref,
           xv, gv, wi, wo, red, prj, later, part, gath, ring, pick, idrow, idxc, idz, where_smem, image_ref, count_ref,
           image_sem, count_sem, x_sem, g_sem, wi_sem, wo_sem, id_send, id_recv, idz_send, idz_recv,
           p1_send, p1_recv, ag_send, ag_recv, p3_send, p3_recv):
    b, y = lax.axis_index("img"), lax.axis_index("hid")
    z, xc = lax.div(b, XC), lax.rem(b, XC)
    rows, depth = xv.shape
    kw, lw = wi.shape[1], wo.shape[1]
    half_rows, cols = rows // 2, depth // CUTS
    npiece = ny * NEAR
    block, here = lax.div(xc, NEAR), lax.rem(xc, NEAR)
    t = kw // npiece
    slots = 2 * nz * XC
    f32 = jnp.float32

    def at_z(o):
        return (lax.rem(z + o, nz) * XC + xc, y)

    def at_xc(o):
        return lax.rem(xc + o, XC)

    def near(o):
        return lax.rem(here + o, NEAR)

    def to_near(k):
        return z * XC + block * NEAR + k

    def row_part(h):
        return pl.ds(pl.multiple_of(h * half_rows, half_rows), half_rows)

    def col_part(q):
        return pl.ds(pl.multiple_of(q * cols, cols), cols)

    def rows_in(h, q):
        r, c = row_part(h), col_part(q)
        return (
            pltpu.make_async_copy(x_hbm.at[r, c], xv.at[r, c], x_sem.at[h, q]),
            pltpu.make_async_copy(g_hbm.at[r, c], gv.at[r, c], g_sem.at[h, q]),
        )

    def weights_in(q):
        c = col_part(q)
        return (
            pltpu.make_async_copy(wi_hbm.at[c], wi.at[c], wi_sem.at[q]),
            pltpu.make_async_copy(wo_hbm.at[c], wo.at[c], wo_sem.at[q]),
        )

    for q in range(AHEAD):
        (x_in, g_in), (a_in, o_in) = rows_in(0, q), weights_in(q)
        a_in.start()
        x_in.start()
        o_in.start()
        g_in.start()

    image_in = pltpu.make_async_copy(image_hbm, image_ref, image_sem)
    count_in = pltpu.make_async_copy(count_hbm, count_ref, count_sem)
    image_in.start()
    count_in.start()

    barrier = pltpu.get_barrier_semaphore()

    def greet(i, _):
        o = i + 1
        to = (z * XC + lax.rem(xc + lax.rem(o, XC), XC), lax.rem(y + lax.div(o, XC), ny))
        pl.semaphore_signal(barrier, inc=1, device_id=to, device_id_type=MESH)
        return 0

    lax.fori_loop(0, ny * XC - 1, greet, 0)
    for o in range(1, nz):
        pl.semaphore_signal(barrier, inc=1, device_id=at_z(o), device_id_type=MESH)

    later[...] = jnp.zeros_like(later)

    image_in.wait()
    count_in.wait()
    lane = lax.broadcasted_iota(jnp.int32, (8, 128), 1)
    first, second = image_ref[0], image_ref[1]
    idrow[...] = jnp.where(lane == b, first + 1, jnp.where(lane == slots // 2 + b, second + 1, 0))
    c0, c1 = count_ref[0], count_ref[1]

    def sketch(a, projected, h, start, count):
        pos = lax.broadcasted_iota(jnp.int32, (half_rows, lw), 0) + h * half_rows
        hi, lo = split(jnp.where((pos >= start) & (pos < start + count), projected, 0.0))
        full = jnp.dot(a, jnp.concatenate([hi, lo], axis=1), preferred_element_type=f32)
        return full[:kw, :lw] + (full[:kw, lw:] + full[kw:, :lw])

    def side_of(yy):
        return lax.div(yy, 2)

    def quarter(yy):
        return yy

    def send_piece(s, k, yy):
        pltpu.make_async_remote_copy(
            src_ref=part.at[s, quarter(yy) * NEAR + k], dst_ref=gath.at[s, y, here],
            send_sem=p1_send.at[s], recv_sem=p1_recv.at[s, here],
            device_id=(to_near(k), yy), device_id_type=MESH).start()

    def half(h, _):
        def arrive(q):
            for c in rows_in(h, q):
                c.wait()

            @pl.when(h == 0)
            def _():
                for c in weights_in(q):
                    c.wait()

            n = h * CUTS + q + AHEAD

            @pl.when(n < 2 * CUTS)
            def _():
                hh, qq = lax.div(n, CUTS), lax.rem(n, CUTS)

                @pl.when(hh == 0)
                def _():
                    for c in weights_in(qq):
                        c.start()

                for c in rows_in(hh, qq):
                    c.start()

        def products(q):
            r, c = row_part(h), col_part(q)
            return (
                red[...] + jnp.dot(xv[r, c], wi[c, :], preferred_element_type=f32),
                prj[...] + jnp.dot(gv[r, c], wo[c, :], preferred_element_type=f32),
            )

        def step(q, _):
            arrive(q)
            red[...], prj[...] = products(q)
            return 0

        red[...] = jnp.zeros_like(red)
        prj[...] = jnp.zeros_like(prj)
        lax.fori_loop(0, CUTS - 1, step, 0)
        arrive(CUTS - 1)
        reduced, projected = products(CUTS - 1)
        a = jnp.concatenate(split(reduced.T), axis=0)
        value = later[...] + sketch(a, projected, h, jnp.where(h == 0, 0, c0), jnp.where(h == 0, c0, c1))
        for i in range(npiece):
            part[h, i] = value[i * t : (i + 1) * t]

        @pl.when(h == 0)
        def _():
            pl.semaphore_wait(barrier, ny * XC + nz - 2)

        def to_row(yy, _):
            for o in far_first(NEAR):
                send_piece(h, near(o), yy)

            @pl.when(yy != y)
            def _():
                send_piece(h, here, yy)

            return 0

        lax.fori_loop(0, ny, to_row, 0)
        pltpu.make_async_copy(part.at[h, quarter(y) * NEAR + here], gath.at[h, y, here], p1_recv.at[h, here]).start()

        @pl.when(h == 0)
        def _():
            for o in far_first(NEAR):
                pltpu.make_async_remote_copy(
                    src_ref=idrow, dst_ref=idxc.at[here], send_sem=id_send, recv_sem=id_recv,
                    device_id=(to_near(near(o)), y), device_id_type=MESH).start()
            idxc[here] = idrow[...]
            later[...] = sketch(a, projected, 0, c0, c1)

        return 0

    lax.fori_loop(0, 2, half, 0)

    def others_z(j):
        return j + jnp.where(j >= z, 1, 0)

    def spread(s):
        for k in range(NEAR):
            pltpu.make_async_copy(gath.at[s, :, 0], gath.at[s, :, 0], p1_recv.at[s, k]).wait()
        total = gath[s, 0]
        for i in range(1, ny):
            total = total + gath[s, i]
        ring[s, z] = total

        def to_z(j, _):
            pltpu.make_async_remote_copy(
                src_ref=ring.at[s, z], dst_ref=ring.at[s, z],
                send_sem=ag_send.at[s], recv_sem=ag_recv.at[s],
                device_id=(others_z(j) * XC + xc, y), device_id_type=MESH).start()
            return 0

        lax.fori_loop(0, nz - 1, to_z, 0)

    def add_ids(s, _):
        @pl.when(s == 1)
        def _():
            pltpu.make_async_copy(idxc.at[pl.ds(0, NEAR - 1)], idxc.at[pl.ds(0, NEAR - 1)], id_recv).wait()
            ids = idxc[0]
            for j in range(1, NEAR):
                ids = ids + idxc[j]
            idz[z] = ids
            for o in far_first(nz):
                pltpu.make_async_remote_copy(
                    src_ref=idz.at[z], dst_ref=idz.at[z], send_sem=idz_send, recv_sem=idz_recv,
                    device_id=at_z(o), device_id_type=MESH).start()

        spread(s)
        return 0

    lax.fori_loop(0, 2, add_ids, 0)

    pltpu.make_async_copy(idz.at[pl.ds(0, nz - 1)], idz.at[pl.ds(0, nz - 1)], idz_recv).wait()
    ids = idz[0]
    for j in range(1, nz):
        ids = ids + idz[j]
    for i in range(2 * XC):
        where_smem[i] = jnp.max(jnp.where(ids == 2 * XC * z + i + 1, lane, -1))

    def sent(ref, sem):
        pltpu.make_async_copy(ref, ref, sem).wait()

    sent(idxc.at[pl.ds(0, NEAR - 1)], id_send)
    sent(idz.at[pl.ds(0, nz - 1)], idz_send)
    for s in range(2):
        sent(part.at[s, pl.ds(0, npiece - 1)], p1_send.at[s])
    for s in range(2):
        pltpu.make_async_copy(ring.at[s, pl.ds(0, nz - 1)], ring.at[s, pl.ds(0, nz - 1)], ag_recv.at[s]).wait()

    side = side_of(y)
    place = lax.rem(y, 2) * NEAR + here

    def take(i):
        found = where_smem[i]
        src = jnp.maximum(found, 0)
        piece = ring[lax.div(src, slots // 2), lax.rem(lax.div(src, XC), nz), lax.rem(src, NEAR)]
        pick[i] = jnp.where(found >= 0, piece, 0.0)

    def deliver(i, cc, yy):
        pltpu.make_async_remote_copy(
            src_ref=pick.at[i], dst_ref=out_ref.at[block, place], send_sem=p3_send, recv_sem=p3_recv,
            device_id=(z * XC + cc, yy), device_id_type=MESH).start()

    def to_owner(n, _):
        p, cc = lax.div(n, XC), lax.rem(n, XC)
        i, yy = 2 * cc + p, 2 * p + side
        take(i)

        @pl.when((cc == xc) & (yy == y))
        def _():
            pltpu.make_async_copy(pick.at[i], out_ref.at[block, place], p3_recv).start()

        @pl.when((cc != xc) | (yy != y))
        def _():
            deliver(i, cc, yy)

        return 0

    lax.fori_loop(0, 2 * XC, to_owner, 0)
    for s in range(2):
        sent(ring.at[s, pl.ds(0, nz - 1)], ag_send.at[s])
    own = (y == side) | (y == 2 + side)

    @pl.when(own)
    def _():
        sent(pick.at[pl.ds(0, 2 * XC - 1)], p3_send)

    @pl.when(jnp.logical_not(own))
    def _():
        sent(pick, p3_send)

    pltpu.make_async_copy(out_ref, out_ref, p3_recv).wait()


def body(nz, ny, patches, hidden_grads, proj_in, proj_out, slot_image, patch_counts):
    rows, depth = patches.shape
    hidden = hidden_grads.shape[1]
    kw, lw = proj_in.shape[1], proj_out.shape[1]
    t = kw // (ny * NEAR)
    f32, i32, bf16 = jnp.float32, jnp.int32, jnp.bfloat16
    dma = pltpu.SemaphoreType.DMA
    out = pl.pallas_call(
        functools.partial(kernel, nz, ny),
        out_shape=pltpu.VMEM((XC // NEAR, 2 * NEAR, t, lw), f32),
        in_specs=[pl.BlockSpec(memory_space=pltpu.HBM)] * 6,
        out_specs=pl.BlockSpec(memory_space=pltpu.VMEM),
        scratch_shapes=[
            pltpu.VMEM((rows, depth), bf16), pltpu.VMEM((rows, hidden), bf16),
            pltpu.VMEM((depth, kw), bf16), pltpu.VMEM((hidden, lw), bf16),
            pltpu.VMEM((rows // 2, kw), f32), pltpu.VMEM((rows // 2, lw), f32), pltpu.VMEM((kw, lw), f32),
            pltpu.VMEM((2, ny * NEAR, t, lw), f32),
            pltpu.VMEM((2, ny, NEAR, t, lw), f32),
            pltpu.VMEM((2, nz, NEAR, t, lw), f32),
            pltpu.VMEM((2 * XC, t, lw), f32),
            pltpu.VMEM((8, 128), i32), pltpu.VMEM((NEAR, 8, 128), i32), pltpu.VMEM((nz, 8, 128), i32),
            pltpu.SMEM((2 * XC,), i32), pltpu.SMEM((2,), i32), pltpu.SMEM((2,), i32), dma, dma,
            dma((2, CUTS)), dma((2, CUTS)), dma((CUTS,)), dma((CUTS,)), dma, dma, dma, dma,
            dma((2,)), dma((2, NEAR)), dma((2,)), dma((2,)), dma, dma,
        ],
        name="sketch",
        compiler_params=pltpu.CompilerParams(collective_id=0, has_side_effects=True, vmem_limit_bytes=56 << 20),
    )(slot_image, patch_counts, patches, hidden_grads, proj_in, proj_out)
    return out.reshape(XC // NEAR, 2 * NEAR * t, lw).sum(0)


def solution(mesh):
    ny = mesh.shape["hid"]
    nz = mesh.shape["img"] // XC
    in_specs = (P("img", None), P("img", "hid"), P(), P("hid", None), P("img"), P("img"))
    return jax.shard_map(
        functools.partial(body, nz, ny), mesh=mesh, in_specs=in_specs,
        out_specs=P(("img", "hid"), None), check_vma=False)
```
